1024 devices in a mesh: space: 128 (over x, y, z_hi, core), param: 8 (over z_lo).
Axes of the slice: x: 4, y: 4, z: 32 (z_hi: 4, z_lo: 8; z = z_hi * 8 + z_lo), core: 2. Of those that a mesh axis runs over, the one named last changes fastest.
Arguments:
- grain_param: int32 [128, 8, 8, 128], P('space'), may hold values from 0 to 127, as said below
- perturbation: float32 [128, 128, 8, 8, 128], P('param', 'space'), may hold values from -0.2 to 0.2
- mobility: float32 [128, 8, 8, 128], P('space'), may hold values from 0.25 to 2.5
Outputs:
- fields: float32 [128, 128, 8, 8, 128], P('param', 'space')
The draws below stay inside these ranges and needn't reach their ends.
Inputs may be any that keep to these rules, and one draw needn't show every extreme that they name: `grain_param`: in the grid, constant on aligned blocks of 2 x 2 x 4 cells; every one of the 128 order parameters is the value of some block.
All inputs are finite; a program needn't handle non-finite values.
Results may differ from the reference program's by a relative error of at most 0.0003.
Values sent between devices are 32-bit elements; how exact they have to be, the bound alone decides.
A program may use at most 32 MiB of HBM per device.

```python
import math
import jax
import jax.numpy as jnp
from jax import lax

P_SIZE = 128
CX = 8
CY = 8
NZ = 128
OUTER = 2
SUB = 2
TILES = 128
NX = 8
NY = 1024


def draw_grain_param(key, part):
    blocks = NX // 2 * (NY // 2) * (NZ // 4)
    labels = jax.random.permutation(key, blocks).astype(jnp.int32) % P_SIZE
    coarse = labels.reshape(NX // 2, NY // 2, NZ // 4)
    coarse = jnp.repeat(coarse, 2, axis=0)
    coarse = jnp.repeat(coarse, 2, axis=1)
    coarse = jnp.repeat(coarse, 4, axis=2)
    tiled = coarse.reshape(NX, TILES, CY, NZ).transpose(1, 0, 2, 3)
    return tiled.astype(jnp.int32)


def block_scale(stream_key, dims, split, least, high):
    level = 1.0
    for axis_at, blocks in split:
        steps = jax.random.uniform(jax.random.fold_in(jax.random.fold_in(stream_key, 6), axis_at), (blocks,), jnp.float32, least / len(split), high / len(split))
        level = level * jnp.repeat(jnp.exp(steps), dims[axis_at] // blocks).reshape((-1,) + (1,) * (len(dims) - 1 - axis_at))
    return level


def normal_values(stream_key, shape, deviation, most, split=(), kind=jnp.bfloat16):
    gain = block_scale(stream_key, shape, split, -0.22, 0.18) if split else 1.0
    entries = jax.random.normal(stream_key, shape, jnp.float32) * deviation * gain
    return jnp.minimum(jnp.maximum(entries, -most), most).astype(kind)


def setup_inputs(seed: int = 0) -> dict:
    key_of = jax.random.split(jax.random.key(seed), 4)
    grain_param = draw_grain_param(jax.random.fold_in(key_of[3], 71), 0)
    perturbation = normal_values(key_of[1], (P_SIZE, TILES, CX, CY, NZ), 0.04, 0.2, ((0, 8), (1, 128)), jnp.float32)
    mobility = jnp.clip(jnp.exp(math.log(2.5) - 2.3025851 * jax.random.uniform(key_of[2], (TILES, CX, CY, NZ), jnp.float32) ** block_scale(key_of[2], (TILES, CX, CY, NZ), ((0, 128),), -0.2, 0.2)), 0.25, 2.5)
    return dict(grain_param=grain_param, perturbation=perturbation, mobility=mobility)


time_step = 0.05
cross_weight = 1.5


def to_grid(block):
    return block.transpose(1, 0, 2, 3).reshape(NX, NY, NZ)


def to_tiles(grid):
    return grid.reshape(NX, TILES, CY, NZ).transpose(1, 0, 2, 3)


def divergence(values, mobility):
    summed = jnp.zeros_like(values)
    for dimension in range(3):
        extent = values.shape[dimension]
        layout = [1, 1, 1]
        layout[dimension] = extent
        open_face = (jnp.arange(extent) < extent - 1).astype(values.dtype).reshape(layout)
        forward = jnp.roll(values, -1, dimension)
        face_mobility = 0.5 * (mobility + jnp.roll(mobility, -1, dimension)) * open_face
        flow_rate = face_mobility * (forward - values)
        summed = summed + flow_rate - jnp.roll(flow_rate, 1, dimension)
    return summed


def advance(values, mobility, totals):
    reaction = values * values * values - values + 2.0 * cross_weight * values * (totals - values * values)
    return values + time_step * (divergence(values, mobility) - mobility * reaction)


def reference(grain_param, perturbation, mobility):
    labels = jnp.arange(P_SIZE, dtype=jnp.int32)

    def initial(pair):
        return jnp.where(grain_param == pair[0], 1.0, 0.0).astype(perturbation.dtype) + pair[1]

    fields = lax.map(initial, (labels, perturbation))
    mobility_grid = to_grid(mobility)
    for _ in range(OUTER):
        totals = to_grid(jnp.sum(fields * fields, axis=0))

        def evolve(block):
            grid = to_grid(block)
            for _ in range(SUB):
                grid = advance(grid, mobility_grid, totals)
            return to_tiles(grid)

        fields = lax.map(evolve, fields)
    return fields
```

```python
import functools
import jax
import jax.numpy as jnp
from jax import lax
from jax.experimental import pallas as pl
from jax.experimental.pallas import tpu as pltpu
from jax.sharding import PartitionSpec as P

MESH = pl.DeviceIdType.MESH
DT = 0.05
H0 = 3
OWNERS = (2, 3, 4, 5)


def kernel(nspace, nparam, g_hbm, u_hbm, m_hbm, out, *scratch):
    (G, U, MI, F0, F1, F2, F3, M, HX, HZ, HY, S0, S1, RS0, RS1, T0, T1,
     in_sem, m_s, m_r, h0_s, h0_r, h2_s, h2_r,
     rs0_s, rs0_r, rs1_s, rs1_r, ag0_s, ag0_r, ag1_s, ag1_r, ex0_s, ex0_r, ex1_s, ex1_r) = scratch
    cx, ny, nz = 8, 8, 128
    count = F0.shape[1]
    own = len(OWNERS)
    span = ny // own
    s = lax.axis_index("space")
    p = lax.axis_index("param")
    up = lax.rem(s + 1, nspace)
    down = lax.rem(s + nspace - 1, nspace)

    loads = [
        pltpu.make_async_copy(g_hbm, G, in_sem.at[0]),
        pltpu.make_async_copy(m_hbm, MI, in_sem.at[1]),
        pltpu.make_async_copy(u_hbm, U, in_sem.at[2]),
    ]
    for load in loads:
        load.start()

    barrier = pltpu.get_barrier_semaphore()

    def greet(device):
        pl.semaphore_signal(barrier, inc=1, device_id=device, device_id_type=MESH)

    for k in range(1, nparam):
        greet((s, lax.rem(p + k, nparam)))
    greet((up, p))
    greet((down, p))
    greet((up, OWNERS[0]))
    greet((down, OWNERS[-1]))

    loads[0].wait()
    loads[1].wait()
    for j in range(ny):
        M[j + H0] = MI[pl.ds(j, cx, stride=ny), :]
    loads[2].wait()
    for j in range(ny):
        label = G[pl.ds(j, cx, stride=ny), :] - p * count
        total = None
        for q in range(count):
            value = U[pl.ds(q * cx * ny + j, cx, stride=ny), :]
            value = jnp.where(label == q, 1.0, 0.0) + value
            F0[j + H0, q] = value
            total = value * value if total is None else total + value * value
        S0[j] = total

    is_ender = jnp.logical_or(p == OWNERS[0], p == OWNERS[-1])

    @pl.when(is_ender)
    def _():
        pl.semaphore_wait(barrier, nparam + 1 + nparam)

    @pl.when(jnp.logical_not(is_ender))
    def _():
        pl.semaphore_wait(barrier, nparam + 1)

    def remote(src, dst, send, recv, device):
        return pltpu.make_async_remote_copy(
            src_ref=src, dst_ref=dst, send_sem=send, recv_sem=recv,
            device_id=device, device_id_type=MESH)

    def reduce_copy(S, RS, ss, rr, i, slot):
        return remote(S.at[pl.ds(i * span, span)], RS.at[slot], ss.at[i], rr.at[slot], (s, OWNERS[i]))

    def reduce_start(S, RS, ss, rr):
        for i in range(own):
            @pl.when(p != OWNERS[i])
            def _():
                reduce_copy(S, RS, ss, rr, i, p).start()

    def group_copy(T, edge, ss, rr, i, q):
        rows = T.at[pl.ds(edge + i * span, span)]
        return remote(rows, rows, ss.at[q], rr.at[i], (s, q))

    def edge_copy(T, edge, ss, rr, side, q):
        if side == 0:
            return remote(T.at[pl.ds(ny, edge)], T.at[pl.ds(0, edge)], ss.at[q], rr.at[0], (up, q))
        return remote(T.at[pl.ds(edge, edge)], T.at[pl.ds(edge + ny, edge)], ss.at[q], rr.at[1], (down, q))

    def finish_totals(S, RS, rs_s, rs_r, T, edge, ag_s, ag_r, ex_s, ex_r):
        for i in range(own):
            @pl.when(p == OWNERS[i])
            def _():
                total = S[pl.ds(i * span, span)]
                for q in range(nparam):
                    if q != OWNERS[i]:
                        reduce_copy(S, RS, rs_s, rs_r, i, q).wait_recv()
                        total = total + RS[q]
                T[pl.ds(edge + i * span, span)] = total
                if i == own - 1:
                    for q in range(nparam):
                        edge_copy(T, edge, ex_s, ex_r, 0, q).start()
                if i == 0:
                    for q in reversed(range(nparam)):
                        edge_copy(T, edge, ex_s, ex_r, 1, q).start()
                for d in reversed(range(1, nparam)):
                    for q in (OWNERS[i] - d, OWNERS[i] + d):
                        if 0 <= q < nparam:
                            group_copy(T, edge, ag_s, ag_r, i, q).start()

    def group_wait(T, edge, ag_s, ag_r):
        for i in range(own):
            @pl.when(p != OWNERS[i])
            def _():
                group_copy(T, edge, ag_s, ag_r, i, 0).wait_recv()

    def edge_wait(T, edge, ex_s, ex_r):
        for side in (0, 1):
            edge_copy(T, edge, ex_s, ex_r, side, 0).wait_recv()

    def settle(S, RS, rs_s, rs_r, T, edge, ag_s, ag_r, ex_s, ex_r):
        for i in range(own):
            @pl.when(p != OWNERS[i])
            def _():
                reduce_copy(S, RS, rs_s, rs_r, i, p).wait_send()

            @pl.when(p == OWNERS[i])
            def _():
                for q in range(nparam):
                    if q != OWNERS[i]:
                        group_copy(T, edge, ag_s, ag_r, i, q).wait_send()
                    if i == own - 1:
                        edge_copy(T, edge, ex_s, ex_r, 0, q).wait_send()
                    if i == 0:
                        edge_copy(T, edge, ex_s, ex_r, 1, q).wait_send()

    def halo_pair(F, halo, ss, rr, k):
        return (
            remote(F.at[halo + ny - 1 - k], F.at[halo - 1 - k], ss.at[0, k], rr.at[0, k], (up, p)),
            remote(F.at[halo + k], F.at[halo + ny + k], ss.at[1, k], rr.at[1, k], (down, p)),
        )

    mobility = (
        remote(M.at[pl.ds(ny, H0)], M.at[pl.ds(0, H0)], m_s.at[0], m_r.at[0], (up, p)),
        remote(M.at[pl.ds(H0, H0)], M.at[pl.ds(H0 + ny, H0)], m_s.at[1], m_r.at[1], (down, p)),
    )
    first = [halo_pair(F0, H0, h0_s, h0_r, k) for k in range(H0)]
    second = {k: halo_pair(F2, 2, h2_s, h2_r, k) for k in range(H0 - 2, 2)}

    sum0 = (S0, RS0, rs0_s, rs0_r, T0, H0 - 1, ag0_s, ag0_r, ex0_s, ex0_r)
    sum1 = (S1, RS1, rs1_s, rs1_r, T1, 1, ag1_s, ag1_r, ex1_s, ex1_r)

    reduce_start(S0, RS0, rs0_s, rs0_r)
    for copy in mobility:
        copy.start()
    for pair in first:
        for copy in pair:
            copy.start()

    below = jnp.where(s > 0, 0.5 * DT, 0.0)
    above = jnp.where(s < nspace - 1, 0.5 * DT, 0.0)
    inner_x = jnp.where(lax.broadcasted_iota(jnp.int32, (cx, nz), 0) < cx - 1, 0.5 * DT, 0.0)
    inner_z = jnp.where(lax.broadcasted_iota(jnp.int32, (cx, nz), 1) < nz - 1, 0.5 * DT, 0.0)

    def row_faces(y):
        m = M[y + H0]
        HX[y + H0 - 1] = inner_x * (m + pltpu.roll(m, cx - 1, 0))
        HZ[y + H0 - 1] = inner_z * (m + pltpu.roll(m, nz - 1, 1))

    def column_face(y):
        scale = below if y == -1 else above if y == ny - 1 else 0.5 * DT
        HY[y + H0] = scale * (M[y + H0] + M[y + H0 + 1])

    for y in range(ny):
        row_faces(y)
    for y in range(ny - 1):
        column_face(y)

    def advance(src, so, store, T, edge, lo, hi, S=None):
        def row(y, carry):
            m = M[y + H0]
            linear = 1.0 - (DT * m) * (3.0 * T[y + edge] - 1.0)
            square = (2.0 * DT) * m
            hx = HX[y + H0 - 1]
            hz = HZ[y + H0 - 1]
            hu = HY[y + H0]
            hl = HY[y + H0 - 1]
            total = None
            for q in range(count):
                f = src[y + so, q]
                gx = hx * (pltpu.roll(f, cx - 1, 0) - f)
                gz = hz * (pltpu.roll(f, nz - 1, 1) - f)
                flow = hu * (src[y + so + 1, q] - f) - hl * (f - src[y + so - 1, q])
                flow = flow + ((gx - pltpu.roll(gx, 1, 0)) + (gz - pltpu.roll(gz, 1, 1)))
                value = f * (linear + square * (f * f)) + flow
                store(y, q, value)
                if S is not None:
                    total = value * value if total is None else total + value * value
            if S is not None:
                S[y] = total
            return carry

        if hi - lo == 1:
            row(lo, 0)
        else:
            lax.fori_loop(lo, hi, row, 0)

    def into(F, halo):
        def store(y, q, value):
            F[y + halo, q] = value
        return store

    def emit(y, q, value):
        out[pl.ds(q * cx * ny + y, cx, stride=ny), :] = value

    step1 = functools.partial(advance, F0, H0, into(F1, H0 - 1), T0, H0 - 1)
    step2 = functools.partial(advance, F1, H0 - 1, into(F2, 2), T0, H0 - 1)
    step3 = functools.partial(advance, F2, 2, into(F3, 1), T1, 1)
    step4 = functools.partial(advance, F3, 1, emit, T1, 1)

    finish_totals(*sum0)
    for copy in mobility:
        copy.wait_recv()
    for k in range(H0 - 1):
        row_faces(-1 - k)
        row_faces(ny + k)
    for k in range(H0):
        column_face(-1 - k)
        column_face(ny - 1 + k)

    group_wait(T0, H0 - 1, ag0_s, ag0_r)
    step1(1, ny - 1)
    step2(2, ny - 2, S1)
    for copy in first[0]:
        copy.wait_recv()
    step1(0, 1)
    step1(ny - 1, ny)
    step2(1, 2, S1)
    step2(ny - 2, ny - 1, S1)
    edge_wait(T0, H0 - 1, ex0_s, ex0_r)
    for copy in first[1]:
        copy.wait_recv()
    step1(-1, 0)
    step1(ny, ny + 1)
    step2(0, 1, S1)
    step2(ny - 1, ny, S1)

    reduce_start(S1, RS1, rs1_s, rs1_r)
    for k in second:
        for copy in second[k]:
            copy.start()
    finish_totals(*sum1)
    for k in range(2, H0):
        for copy in first[k]:
            copy.wait_recv()
        step1(-k, 1 - k)
        step1(ny + k - 1, ny + k)
        step2(1 - k, 2 - k)
        step2(ny + k - 2, ny + k - 1)

    group_wait(T1, 1, ag1_s, ag1_r)
    step3(1, ny - 1)
    step4(2, ny - 2)
    if 0 in second:
        for copy in second[0]:
            copy.wait_recv()
    step3(0, 1)
    step3(ny - 1, ny)
    step4(1, 2)
    step4(ny - 2, ny - 1)
    edge_wait(T1, 1, ex1_s, ex1_r)
    if 1 in second:
        for copy in second[1]:
            copy.wait_recv()
    step3(-1, 0)
    step3(ny, ny + 1)
    step4(0, 1)
    step4(ny - 1, ny)

    for copy in mobility:
        copy.wait_send()
    for pair in first + list(second.values()):
        for copy in pair:
            copy.wait_send()
    settle(*sum0)
    settle(*sum1)


def local(nspace, nparam, grain_param, perturbation, mobility):
    count, _, cx, ny, nz = perturbation.shape
    own = len(OWNERS)
    f32 = jnp.float32
    row = (cx, nz)
    hbm = pl.BlockSpec(memory_space=pltpu.HBM)
    dma = pltpu.SemaphoreType.DMA
    sums = [dma((own,)), dma((nparam,))] * 2 + [dma((nparam,)), dma((own,))] * 2 + [dma((nparam,)), dma((2,))] * 2
    out = pl.pallas_call(
        functools.partial(kernel, nspace, nparam),
        out_shape=jax.ShapeDtypeStruct((count * cx * ny, nz), f32),
        in_specs=[hbm] * 3,
        out_specs=pl.BlockSpec(memory_space=pltpu.VMEM),
        scratch_shapes=[
            pltpu.VMEM((cx * ny, nz), jnp.int32),
            pltpu.VMEM((count * cx * ny, nz), f32),
            pltpu.VMEM((cx * ny, nz), f32),
            pltpu.VMEM((ny + 2 * H0, count) + row, f32),
            pltpu.VMEM((ny + 2 * H0 - 2, count) + row, f32),
            pltpu.VMEM((ny + 4, count) + row, f32),
            pltpu.VMEM((ny + 2, count) + row, f32),
            pltpu.VMEM((ny + 2 * H0,) + row, f32),
            pltpu.VMEM((ny + 2 * H0 - 2,) + row, f32),
            pltpu.VMEM((ny + 2 * H0 - 2,) + row, f32),
            pltpu.VMEM((ny + 2 * H0 - 1,) + row, f32),
            pltpu.VMEM((ny,) + row, f32),
            pltpu.VMEM((ny,) + row, f32),
            pltpu.VMEM((nparam, ny // own) + row, f32),
            pltpu.VMEM((nparam, ny // own) + row, f32),
            pltpu.VMEM((ny + 2 * H0 - 2,) + row, f32),
            pltpu.VMEM((ny + 2,) + row, f32),
            dma((3,)),
            dma((2,)), dma((2,)),
            dma((2, H0)), dma((2, H0)),
            dma((2, 2)), dma((2, 2)),
        ] + sums,
        compiler_params=pltpu.CompilerParams(
            collective_id=0, has_side_effects=True, vmem_limit_bytes=32 << 20),
        cost_estimate=pl.CostEstimate(flops=12_000_000, bytes_accessed=1_200_000, transcendentals=0),
    )(
        grain_param.reshape(cx * ny, nz),
        perturbation.reshape(count * cx * ny, nz),
        mobility.reshape(cx * ny, nz),
    )
    return out.reshape(perturbation.shape)


def solution(mesh):
    nspace, nparam = mesh.shape["space"], mesh.shape["param"]
    in_specs = (
        P("space", None, None, None),
        P("param", "space", None, None, None),
        P("space", None, None, None),
    )
    out_specs = P("param", "space", None, None, None)
    return jax.shard_map(
        functools.partial(local, nspace, nparam), mesh=mesh, in_specs=in_specs, out_specs=out_specs, check_vma=False)
```

```python
import functools
import jax
import jax.numpy as jnp
from jax import lax
from jax.experimental import pallas as pl
from jax.experimental.pallas import tpu as pltpu
from jax.sharding import PartitionSpec as P

MESH = pl.DeviceIdType.MESH
DT = 0.05
H0 = 2
OWNERS = (2, 3, 4, 5)


def kernel(nspace, nparam, g_hbm, u_hbm, m_hbm, out, *scratch):
    (G, U, MI, F0, F1, F2, F3, M, HX, HZ, HY, S0, S1, RS0, RS1, T0, T1,
     in_sem, m_s, m_r, h0_s, h0_r, h2_s, h2_r,
     rs0_s, rs0_r, rs1_s, rs1_r, ag0_s, ag0_r, ag1_s, ag1_r, ex0_s, ex0_r, ex1_s, ex1_r) = scratch
    cx, ny, nz = 8, 8, 128
    count = F0.shape[1]
    own = len(OWNERS)
    span = ny // own
    s = lax.axis_index("space")
    p = lax.axis_index("param")
    up = lax.rem(s + 1, nspace)
    down = lax.rem(s + nspace - 1, nspace)
    sides = (s < nspace - 1, s > 0)
    up_count = jnp.where(sides[0], 1, 0)
    down_count = jnp.where(sides[1], 1, 0)

    loads = [
        pltpu.make_async_copy(g_hbm, G, in_sem.at[0]),
        pltpu.make_async_copy(m_hbm, MI, in_sem.at[1]),
        pltpu.make_async_copy(u_hbm, U, in_sem.at[2]),
    ]
    for load in loads:
        load.start()

    barrier = pltpu.get_barrier_semaphore()

    def greet(device):
        pl.semaphore_signal(barrier, inc=1, device_id=device, device_id_type=MESH)

    for k in range(1, nparam):
        greet((s, lax.rem(p + k, nparam)))

    @pl.when(sides[0])
    def _():
        greet((up, p))
        greet((up, OWNERS[0]))

    @pl.when(sides[1])
    def _():
        greet((down, p))
        greet((down, OWNERS[-1]))

    loads[0].wait()
    loads[1].wait()
    for j in range(ny):
        M[j + H0] = MI[pl.ds(j, cx, stride=ny), :]
    loads[2].wait()
    for j in range(ny):
        label = G[pl.ds(j, cx, stride=ny), :] - p * count
        total = None
        for q in range(count):
            value = U[pl.ds(q * cx * ny + j, cx, stride=ny), :]
            value = jnp.where(label == q, 1.0, 0.0) + value
            F0[j + H0, q] = value
            total = value * value if total is None else total + value * value
        S0[j] = total

    def blank(low, refs):
        for ref, halo in refs:
            for k in range(halo):
                row = ref.at[halo - 1 - k] if low else ref.at[halo + ny + k]
                row[...] = jnp.zeros_like(row)

    beyond = ((F0, H0), (F2, 2), (M, H0), (T0, H0 - 1), (T1, 1))

    @pl.when(jnp.logical_not(sides[1]))
    def _():
        blank(True, beyond)

    @pl.when(jnp.logical_not(sides[0]))
    def _():
        blank(False, beyond)

    heard = nparam - 1 + up_count + down_count
    heard = heard + jnp.where(p == OWNERS[0], nparam, 0) * down_count
    heard = heard + jnp.where(p == OWNERS[-1], nparam, 0) * up_count
    pl.semaphore_wait(barrier, heard)

    def remote(src, dst, send, recv, device):
        return pltpu.make_async_remote_copy(
            src_ref=src, dst_ref=dst, send_sem=send, recv_sem=recv,
            device_id=device, device_id_type=MESH)

    def start_sided(copies):
        for side in (0, 1):
            @pl.when(sides[side])
            def _():
                copies[side].start()

    def sent_sided(copies):
        for side in (0, 1):
            @pl.when(sides[side])
            def _():
                copies[side].wait_send()

    def arrived_sided(copies):
        for side in (0, 1):
            @pl.when(sides[1 - side])
            def _():
                copies[side].wait_recv()

    def reduce_copy(S, RS, ss, rr, i, slot):
        return remote(S.at[pl.ds(i * span, span)], RS.at[slot], ss.at[i], rr.at[slot], (s, OWNERS[i]))

    def reduce_start(S, RS, ss, rr, which=range(own)):
        for i in which:
            @pl.when(p != OWNERS[i])
            def _():
                reduce_copy(S, RS, ss, rr, i, p).start()

    def group_copy(T, edge, ss, rr, i, q):
        rows = T.at[pl.ds(edge + i * span, span)]
        return remote(rows, rows, ss.at[q], rr.at[i], (s, q))

    def edge_copy(T, edge, ss, rr, side, q):
        if side == 0:
            return remote(T.at[pl.ds(ny, edge)], T.at[pl.ds(0, edge)], ss.at[q], rr.at[0], (up, q))
        return remote(T.at[pl.ds(edge, edge)], T.at[pl.ds(edge + ny, edge)], ss.at[q], rr.at[1], (down, q))

    def finish_totals(S, RS, rs_s, rs_r, T, edge, ag_s, ag_r, ex_s, ex_r):
        for i in range(own):
            @pl.when(p == OWNERS[i])
            def _():
                total = S[pl.ds(i * span, span)]
                for q in range(nparam):
                    if q != OWNERS[i]:
                        reduce_copy(S, RS, rs_s, rs_r, i, q).wait_recv()
                        total = total + RS[q]
                T[pl.ds(edge + i * span, span)] = total
                if i == own - 1:
                    @pl.when(sides[0])
                    def _():
                        for q in range(nparam):
                            edge_copy(T, edge, ex_s, ex_r, 0, q).start()
                if i == 0:
                    @pl.when(sides[1])
                    def _():
                        for q in reversed(range(nparam)):
                            edge_copy(T, edge, ex_s, ex_r, 1, q).start()
                for d in reversed(range(1, nparam)):
                    for q in (OWNERS[i] - d, OWNERS[i] + d):
                        if 0 <= q < nparam:
                            group_copy(T, edge, ag_s, ag_r, i, q).start()

    def group_wait(T, edge, ag_s, ag_r):
        for i in range(own):
            @pl.when(p != OWNERS[i])
            def _():
                group_copy(T, edge, ag_s, ag_r, i, 0).wait_recv()

    def edge_wait(T, edge, ex_s, ex_r):
        arrived_sided([edge_copy(T, edge, ex_s, ex_r, side, 0) for side in (0, 1)])

    def settle(S, RS, rs_s, rs_r, T, edge, ag_s, ag_r, ex_s, ex_r):
        for i in range(own):
            @pl.when(p != OWNERS[i])
            def _():
                reduce_copy(S, RS, rs_s, rs_r, i, p).wait_send()

            @pl.when(p == OWNERS[i])
            def _():
                for q in range(nparam):
                    if q != OWNERS[i]:
                        group_copy(T, edge, ag_s, ag_r, i, q).wait_send()
                for side, j in ((0, own - 1), (1, 0)):
                    if i == j:
                        @pl.when(sides[side])
                        def _():
                            for q in range(nparam):
                                edge_copy(T, edge, ex_s, ex_r, side, q).wait_send()

    def halo_pair(F, halo, ss, rr, k):
        return (
            remote(F.at[halo + ny - 1 - k], F.at[halo - 1 - k], ss.at[0, k], rr.at[0, k], (up, p)),
            remote(F.at[halo + k], F.at[halo + ny + k], ss.at[1, k], rr.at[1, k], (down, p)),
        )

    mobility = (
        remote(M.at[pl.ds(ny, H0)], M.at[pl.ds(0, H0)], m_s.at[0], m_r.at[0], (up, p)),
        remote(M.at[pl.ds(H0, H0)], M.at[pl.ds(H0 + ny, H0)], m_s.at[1], m_r.at[1], (down, p)),
    )
    first = [halo_pair(F0, H0, h0_s, h0_r, k) for k in range(H0)]
    second = {k: halo_pair(F2, 2, h2_s, h2_r, k) for k in range(H0 - 2, 2)}

    sum0 = (S0, RS0, rs0_s, rs0_r, T0, H0 - 1, ag0_s, ag0_r, ex0_s, ex0_r)
    sum1 = (S1, RS1, rs1_s, rs1_r, T1, 1, ag1_s, ag1_r, ex1_s, ex1_r)

    reduce_start(S0, RS0, rs0_s, rs0_r)
    start_sided(mobility)
    start_sided(first[0])

    start_sided(first[1])

    below = jnp.where(s > 0, 0.5 * DT, 0.0)
    above = jnp.where(s < nspace - 1, 0.5 * DT, 0.0)
    inner_x = jnp.where(lax.broadcasted_iota(jnp.int32, (cx, nz), 0) < cx - 1, 0.5 * DT, 0.0)
    inner_z = jnp.where(lax.broadcasted_iota(jnp.int32, (cx, nz), 1) < nz - 1, 0.5 * DT, 0.0)

    def row_faces(y):
        m = M[y + H0]
        HX[y + H0 - 1] = inner_x * (m + pltpu.roll(m, cx - 1, 0))
        HZ[y + H0 - 1] = inner_z * (m + pltpu.roll(m, nz - 1, 1))

    def column_face(y):
        scale = below if y == -1 else above if y == ny - 1 else 0.5 * DT
        HY[y + H0] = scale * (M[y + H0] + M[y + H0 + 1])

    for y in range(ny):
        row_faces(y)
    for y in range(ny - 1):
        column_face(y)

    def advance(src, so, store, T, edge, lo, hi, S=None):
        def row(y, carry):
            m = M[y + H0]
            linear = 1.0 - (DT * m) * (3.0 * T[y + edge] - 1.0)
            square = (2.0 * DT) * m
            hx = HX[y + H0 - 1]
            hz = HZ[y + H0 - 1]
            hu = HY[y + H0]
            hl = HY[y + H0 - 1]
            total = None
            for q in range(count):
                f = src[y + so, q]
                gx = hx * (pltpu.roll(f, cx - 1, 0) - f)
                gz = hz * (pltpu.roll(f, nz - 1, 1) - f)
                flow = hu * (src[y + so + 1, q] - f) - hl * (f - src[y + so - 1, q])
                flow = flow + ((gx - pltpu.roll(gx, 1, 0)) + (gz - pltpu.roll(gz, 1, 1)))
                value = f * (linear + square * (f * f)) + flow
                store(y, q, value)
                if S is not None:
                    total = value * value if total is None else total + value * value
            if S is not None:
                S[y] = total
            return carry

        if hi - lo == 1:
            row(lo, 0)
        else:
            lax.fori_loop(lo, hi, row, 0)

    def into(F, halo):
        def store(y, q, value):
            F[y + halo, q] = value
        return store

    def emit(y, q, value):
        out[pl.ds(q * cx * ny + y, cx, stride=ny), :] = value

    step1 = functools.partial(advance, F0, H0, into(F1, H0 - 1), T0, H0 - 1)
    step2 = functools.partial(advance, F1, H0 - 1, into(F2, 2), T0, H0 - 1)
    step3 = functools.partial(advance, F2, 2, into(F3, 1), T1, 1)
    step4 = functools.partial(advance, F3, 1, emit, T1, 1)

    finish_totals(*sum0)

    arrived_sided(mobility)
    for k in range(H0 - 1):
        row_faces(-1 - k)
        row_faces(ny + k)
    for k in range(H0):
        column_face(-1 - k)
        column_face(ny - 1 + k)

    group_wait(T0, H0 - 1, ag0_s, ag0_r)
    step1(1, ny - 1)
    step2(2, ny - 2, S1)
    reduce_start(S1, RS1, rs1_s, rs1_r, (1, 2))
    arrived_sided(first[0])
    step1(0, 1)
    step1(ny - 1, ny)
    step2(1, 2, S1)
    step2(ny - 2, ny - 1, S1)
    start_sided(second[1])
    edge_wait(T0, H0 - 1, ex0_s, ex0_r)
    arrived_sided(first[1])
    step1(-1, 0)
    step1(ny, ny + 1)
    step2(0, 1, S1)
    step2(ny - 1, ny, S1)

    reduce_start(S1, RS1, rs1_s, rs1_r, (0, 3))

    start_sided(second[0])
    finish_totals(*sum1)

    for k in range(2, H0):
        arrived_sided(first[k])
        step1(-k, 1 - k)
        step1(ny + k - 1, ny + k)
        step2(1 - k, 2 - k)
        step2(ny + k - 2, ny + k - 1)

    group_wait(T1, 1, ag1_s, ag1_r)
    step3(1, ny - 1)
    step4(2, ny - 2)
    if 0 in second:
        arrived_sided(second[0])
    step3(0, 1)
    step3(ny - 1, ny)
    step4(1, 2)
    step4(ny - 2, ny - 1)
    edge_wait(T1, 1, ex1_s, ex1_r)
    if 1 in second:
        arrived_sided(second[1])
    step3(-1, 0)
    step3(ny, ny + 1)
    step4(0, 1)
    step4(ny - 1, ny)

    for pair in [mobility] + first + list(second.values()):
        sent_sided(pair)
    settle(*sum0)
    settle(*sum1)


def local(nspace, nparam, grain_param, perturbation, mobility):
    count, _, cx, ny, nz = perturbation.shape
    own = len(OWNERS)
    f32 = jnp.float32
    row = (cx, nz)
    hbm = pl.BlockSpec(memory_space=pltpu.HBM)
    dma = pltpu.SemaphoreType.DMA
    sums = [dma((own,)), dma((nparam,))] * 2 + [dma((nparam,)), dma((own,))] * 2 + [dma((nparam,)), dma((2,))] * 2
    out = pl.pallas_call(
        functools.partial(kernel, nspace, nparam),
        out_shape=jax.ShapeDtypeStruct((count * cx * ny, nz), f32),
        in_specs=[hbm] * 3,
        out_specs=pl.BlockSpec(memory_space=pltpu.VMEM),
        scratch_shapes=[
            pltpu.VMEM((cx * ny, nz), jnp.int32),
            pltpu.VMEM((count * cx * ny, nz), f32),
            pltpu.VMEM((cx * ny, nz), f32),
            pltpu.VMEM((ny + 2 * H0, count) + row, f32),
            pltpu.VMEM((ny + 2 * H0 - 2, count) + row, f32),
            pltpu.VMEM((ny + 4, count) + row, f32),
            pltpu.VMEM((ny + 2, count) + row, f32),
            pltpu.VMEM((ny + 2 * H0,) + row, f32),
            pltpu.VMEM((ny + 2 * H0 - 2,) + row, f32),
            pltpu.VMEM((ny + 2 * H0 - 2,) + row, f32),
            pltpu.VMEM((ny + 2 * H0 - 1,) + row, f32),
            pltpu.VMEM((ny,) + row, f32),
            pltpu.VMEM((ny,) + row, f32),
            pltpu.VMEM((nparam, ny // own) + row, f32),
            pltpu.VMEM((nparam, ny // own) + row, f32),
            pltpu.VMEM((ny + 2 * H0 - 2,) + row, f32),
            pltpu.VMEM((ny + 2,) + row, f32),
            dma((3,)),
            dma((2,)), dma((2,)),
            dma((2, H0)), dma((2, H0)),
            dma((2, 2)), dma((2, 2)),
        ] + sums,
        compiler_params=pltpu.CompilerParams(
            collective_id=0, has_side_effects=True, vmem_limit_bytes=60 << 20),
        cost_estimate=pl.CostEstimate(flops=12_000_000, bytes_accessed=1_200_000, transcendentals=0),
    )(
        grain_param.reshape(cx * ny, nz),
        perturbation.reshape(count * cx * ny, nz),
        mobility.reshape(cx * ny, nz),
    )
    return out.reshape(perturbation.shape)


def solution(mesh):
    nspace, nparam = mesh.shape["space"], mesh.shape["param"]
    in_specs = (
        P("space", None, None, None),
        P("param", "space", None, None, None),
        P("space", None, None, None),
    )
    out_specs = P("param", "space", None, None, None)
    return jax.shard_map(
        functools.partial(local, nspace, nparam), mesh=mesh, in_specs=in_specs, out_specs=out_specs, check_vma=False)
```

```python
import functools
import jax
import jax.numpy as jnp
from jax import lax
from jax.experimental import pallas as pl
from jax.experimental.pallas import tpu as pltpu
from jax.sharding import PartitionSpec as P

MESH = pl.DeviceIdType.MESH
DT = 0.05
H0 = 2
OWNERS = (2, 3, 4, 5)
OUT_PARTS = 4


def kernel(nspace, nparam, g_hbm, u_hbm, m_hbm, out_hbm, *scratch):
    (out, out_sem, G, U, MI, F0, F1, F2, F3, M, HX, HZ, HY, S0, S1, RS0, RS1, T0, T1,
     in_sem, m_s, m_r, h0_s, h0_r, h2_s, h2_r,
     rs0_s, rs0_r, rs1_s, rs1_r, ag0_s, ag0_r, ag1_s, ag1_r, ex0_s, ex0_r, ex1_s, ex1_r) = scratch
    cx, ny, nz = 8, 8, 128
    count = F0.shape[1]
    own = len(OWNERS)
    span = ny // own
    s = lax.axis_index("space")
    p = lax.axis_index("param")
    up = lax.rem(s + 1, nspace)
    down = lax.rem(s + nspace - 1, nspace)
    sides = (s < nspace - 1, s > 0)
    up_count = jnp.where(sides[0], 1, 0)
    down_count = jnp.where(sides[1], 1, 0)

    loads = [
        pltpu.make_async_copy(g_hbm, G, in_sem.at[0]),
        pltpu.make_async_copy(m_hbm, MI, in_sem.at[1]),
        pltpu.make_async_copy(u_hbm, U, in_sem.at[2]),
    ]
    for load in loads:
        load.start()

    barrier = pltpu.get_barrier_semaphore()

    def greet(device):
        pl.semaphore_signal(barrier, inc=1, device_id=device, device_id_type=MESH)

    for k in range(1, nparam):
        greet((s, lax.rem(p + k, nparam)))

    @pl.when(sides[0])
    def _():
        greet((up, p))
        greet((up, OWNERS[0]))

    @pl.when(sides[1])
    def _():
        greet((down, p))
        greet((down, OWNERS[-1]))

    loads[0].wait()
    loads[1].wait()
    for j in range(ny):
        M[j + H0] = MI[pl.ds(j, cx, stride=ny), :]
    loads[2].wait()
    for j in range(ny):
        label = G[pl.ds(j, cx, stride=ny), :] - p * count
        total = None
        for q in range(count):
            value = U[pl.ds(q * cx * ny + j, cx, stride=ny), :]
            value = jnp.where(label == q, 1.0, 0.0) + value
            F0[j + H0, q] = value
            total = value * value if total is None else total + value * value
        S0[j] = total

    def blank(low, refs):
        for ref, halo in refs:
            for k in range(halo):
                row = ref.at[halo - 1 - k] if low else ref.at[halo + ny + k]
                row[...] = jnp.zeros_like(row)

    beyond = ((F0, H0), (F2, 2), (M, H0), (T0, H0 - 1), (T1, 1))

    @pl.when(jnp.logical_not(sides[1]))
    def _():
        blank(True, beyond)

    @pl.when(jnp.logical_not(sides[0]))
    def _():
        blank(False, beyond)

    heard = nparam - 1 + up_count + down_count
    heard = heard + jnp.where(p == OWNERS[0], nparam, 0) * down_count
    heard = heard + jnp.where(p == OWNERS[-1], nparam, 0) * up_count
    pl.semaphore_wait(barrier, heard)

    def remote(src, dst, send, recv, device):
        return pltpu.make_async_remote_copy(
            src_ref=src, dst_ref=dst, send_sem=send, recv_sem=recv,
            device_id=device, device_id_type=MESH)

    def start_sided(copies):
        for side in (0, 1):
            @pl.when(sides[side])
            def _():
                copies[side].start()

    def sent_sided(copies):
        for side in (0, 1):
            @pl.when(sides[side])
            def _():
                copies[side].wait_send()

    def arrived_sided(copies):
        for side in (0, 1):
            @pl.when(sides[1 - side])
            def _():
                copies[side].wait_recv()

    def reduce_copy(S, RS, ss, rr, i, slot):
        return remote(S.at[pl.ds(i * span, span)], RS.at[slot], ss.at[i], rr.at[slot], (s, OWNERS[i]))

    def reduce_start(S, RS, ss, rr, which=range(own)):
        for i in which:
            @pl.when(p != OWNERS[i])
            def _():
                reduce_copy(S, RS, ss, rr, i, p).start()

    def group_copy(T, edge, ss, rr, i, q):
        rows = T.at[pl.ds(edge + i * span, span)]
        return remote(rows, rows, ss.at[q], rr.at[i], (s, q))

    def edge_copy(T, edge, ss, rr, side, q):
        if side == 0:
            return remote(T.at[pl.ds(ny, edge)], T.at[pl.ds(0, edge)], ss.at[q], rr.at[0], (up, q))
        return remote(T.at[pl.ds(edge, edge)], T.at[pl.ds(edge + ny, edge)], ss.at[q], rr.at[1], (down, q))

    def finish_totals(S, RS, rs_s, rs_r, T, edge, ag_s, ag_r, ex_s, ex_r):
        for i in range(own):
            @pl.when(p == OWNERS[i])
            def _():
                total = S[pl.ds(i * span, span)]
                for q in range(nparam):
                    if q != OWNERS[i]:
                        reduce_copy(S, RS, rs_s, rs_r, i, q).wait_recv()
                        total = total + RS[q]
                T[pl.ds(edge + i * span, span)] = total
                if i == own - 1:
                    @pl.when(sides[0])
                    def _():
                        for q in range(nparam):
                            edge_copy(T, edge, ex_s, ex_r, 0, q).start()
                if i == 0:
                    @pl.when(sides[1])
                    def _():
                        for q in reversed(range(nparam)):
                            edge_copy(T, edge, ex_s, ex_r, 1, q).start()
                for d in reversed(range(1, nparam)):
                    for q in (OWNERS[i] - d, OWNERS[i] + d):
                        if 0 <= q < nparam:
                            group_copy(T, edge, ag_s, ag_r, i, q).start()

    def group_wait(T, edge, ag_s, ag_r):
        for i in range(own):
            @pl.when(p != OWNERS[i])
            def _():
                group_copy(T, edge, ag_s, ag_r, i, 0).wait_recv()

    def edge_wait(T, edge, ex_s, ex_r):
        arrived_sided([edge_copy(T, edge, ex_s, ex_r, side, 0) for side in (0, 1)])

    def settle(S, RS, rs_s, rs_r, T, edge, ag_s, ag_r, ex_s, ex_r):
        for i in range(own):
            @pl.when(p != OWNERS[i])
            def _():
                reduce_copy(S, RS, rs_s, rs_r, i, p).wait_send()

            @pl.when(p == OWNERS[i])
            def _():
                for q in range(nparam):
                    if q != OWNERS[i]:
                        group_copy(T, edge, ag_s, ag_r, i, q).wait_send()
                for side, j in ((0, own - 1), (1, 0)):
                    if i == j:
                        @pl.when(sides[side])
                        def _():
                            for q in range(nparam):
                                edge_copy(T, edge, ex_s, ex_r, side, q).wait_send()

    def halo_pair(F, halo, ss, rr, k):
        return (
            remote(F.at[halo + ny - 1 - k], F.at[halo - 1 - k], ss.at[0, k], rr.at[0, k], (up, p)),
            remote(F.at[halo + k], F.at[halo + ny + k], ss.at[1, k], rr.at[1, k], (down, p)),
        )

    mobility = (
        remote(M.at[pl.ds(ny, H0)], M.at[pl.ds(0, H0)], m_s.at[0], m_r.at[0], (up, p)),
        remote(M.at[pl.ds(H0, H0)], M.at[pl.ds(H0 + ny, H0)], m_s.at[1], m_r.at[1], (down, p)),
    )
    first = [halo_pair(F0, H0, h0_s, h0_r, k) for k in range(H0)]
    second = {k: halo_pair(F2, 2, h2_s, h2_r, k) for k in range(H0 - 2, 2)}

    sum0 = (S0, RS0, rs0_s, rs0_r, T0, H0 - 1, ag0_s, ag0_r, ex0_s, ex0_r)
    sum1 = (S1, RS1, rs1_s, rs1_r, T1, 1, ag1_s, ag1_r, ex1_s, ex1_r)

    reduce_start(S0, RS0, rs0_s, rs0_r)
    start_sided(mobility)
    start_sided(first[0])

    start_sided(first[1])

    below = jnp.where(s > 0, 0.5 * DT, 0.0)
    above = jnp.where(s < nspace - 1, 0.5 * DT, 0.0)
    inner_x = jnp.where(lax.broadcasted_iota(jnp.int32, (cx, nz), 0) < cx - 1, 0.5 * DT, 0.0)
    inner_z = jnp.where(lax.broadcasted_iota(jnp.int32, (cx, nz), 1) < nz - 1, 0.5 * DT, 0.0)

    def row_faces(y):
        m = M[y + H0]
        HX[y + H0 - 1] = inner_x * (m + pltpu.roll(m, cx - 1, 0))
        HZ[y + H0 - 1] = inner_z * (m + pltpu.roll(m, nz - 1, 1))

    def column_face(y):
        scale = below if y == -1 else above if y == ny - 1 else 0.5 * DT
        HY[y + H0] = scale * (M[y + H0] + M[y + H0 + 1])

    for y in range(ny):
        row_faces(y)
    for y in range(ny - 1):
        column_face(y)

    def advance(src, so, store, T, edge, lo, hi, S=None, fields=None):
        def row(y, carry):
            m = M[y + H0]
            linear = 1.0 - (DT * m) * (3.0 * T[y + edge] - 1.0)
            square = (2.0 * DT) * m
            hx = HX[y + H0 - 1]
            hz = HZ[y + H0 - 1]
            hu = HY[y + H0]
            hl = HY[y + H0 - 1]
            total = None
            for q in fields or range(count):
                f = src[y + so, q]
                gx = hx * (pltpu.roll(f, cx - 1, 0) - f)
                gz = hz * (pltpu.roll(f, nz - 1, 1) - f)
                flow = hu * (src[y + so + 1, q] - f) - hl * (f - src[y + so - 1, q])
                flow = flow + ((gx - pltpu.roll(gx, 1, 0)) + (gz - pltpu.roll(gz, 1, 1)))
                value = f * (linear + square * (f * f)) + flow
                store(y, q, value)
                if S is not None:
                    total = value * value if total is None else total + value * value
            if S is not None:
                S[y] = total
            return carry

        if hi - lo == 1:
            row(lo, 0)
        else:
            lax.fori_loop(lo, hi, row, 0)

    def into(F, halo):
        def store(y, q, value):
            F[y + halo, q] = value
        return store

    def emit(y, q, value):
        out[pl.ds(q * cx * ny + y, cx, stride=ny), :] = value

    step1 = functools.partial(advance, F0, H0, into(F1, H0 - 1), T0, H0 - 1)
    step2 = functools.partial(advance, F1, H0 - 1, into(F2, 2), T0, H0 - 1)
    step3 = functools.partial(advance, F2, 2, into(F3, 1), T1, 1)
    step4 = functools.partial(advance, F3, 1, emit, T1, 1)

    finish_totals(*sum0)

    arrived_sided(mobility)
    for k in range(H0 - 1):
        row_faces(-1 - k)
        row_faces(ny + k)
    for k in range(H0):
        column_face(-1 - k)
        column_face(ny - 1 + k)

    group_wait(T0, H0 - 1, ag0_s, ag0_r)
    step1(1, ny - 1)
    step2(2, ny - 2, S1)
    reduce_start(S1, RS1, rs1_s, rs1_r, (1, 2))
    arrived_sided(first[0])
    step1(0, 1)
    step1(ny - 1, ny)
    step2(1, 2, S1)
    step2(ny - 2, ny - 1, S1)
    start_sided(second[1])
    edge_wait(T0, H0 - 1, ex0_s, ex0_r)
    arrived_sided(first[1])
    step1(-1, 0)
    step1(ny, ny + 1)
    step2(0, 1, S1)
    step2(ny - 1, ny, S1)

    reduce_start(S1, RS1, rs1_s, rs1_r, (0, 3))

    is_owner = functools.reduce(jnp.logical_or, [p == o for o in OWNERS])

    @pl.when(jnp.logical_not(is_owner))
    def _():
        start_sided(second[0])

    finish_totals(*sum1)

    @pl.when(is_owner)
    def _():
        start_sided(second[0])


    for k in range(2, H0):
        arrived_sided(first[k])
        step1(-k, 1 - k)
        step1(ny + k - 1, ny + k)
        step2(1 - k, 2 - k)
        step2(ny + k - 2, ny + k - 1)

    group_wait(T1, 1, ag1_s, ag1_r)
    step3(1, ny - 1)
    step4(2, ny - 2)
    if 0 in second:
        arrived_sided(second[0])
    step3(0, 1)
    step3(ny - 1, ny)
    step4(1, 2)
    step4(ny - 2, ny - 1)
    edge_wait(T1, 1, ex1_s, ex1_r)
    if 1 in second:
        arrived_sided(second[1])
    part = count // OUT_PARTS
    writes = []
    for c in range(OUT_PARTS):
        fields = range(c * part, (c + 1) * part)
        step3(-1, 0, fields=fields)
        step3(ny, ny + 1, fields=fields)
        step4(0, 1, fields=fields)
        step4(ny - 1, ny, fields=fields)
        run = pl.ds(c * part * cx * ny, part * cx * ny)
        write = pltpu.make_async_copy(out.at[run], out_hbm.at[run], out_sem.at[c])
        write.start()
        writes.append(write)

    for pair in [mobility] + first + list(second.values()):
        sent_sided(pair)
    settle(*sum0)
    settle(*sum1)
    for write in writes:
        write.wait()


def local(nspace, nparam, grain_param, perturbation, mobility):
    count, _, cx, ny, nz = perturbation.shape
    own = len(OWNERS)
    f32 = jnp.float32
    row = (cx, nz)
    hbm = pl.BlockSpec(memory_space=pltpu.HBM)
    dma = pltpu.SemaphoreType.DMA
    sums = [dma((own,)), dma((nparam,))] * 2 + [dma((nparam,)), dma((own,))] * 2 + [dma((nparam,)), dma((2,))] * 2
    out = pl.pallas_call(
        functools.partial(kernel, nspace, nparam),
        out_shape=jax.ShapeDtypeStruct((count * cx * ny, nz), f32),
        in_specs=[hbm] * 3,
        out_specs=hbm,
        scratch_shapes=[
            pltpu.VMEM((count * cx * ny, nz), f32),
            dma((OUT_PARTS,)),
            pltpu.VMEM((cx * ny, nz), jnp.int32),
            pltpu.VMEM((count * cx * ny, nz), f32),
            pltpu.VMEM((cx * ny, nz), f32),
            pltpu.VMEM((ny + 2 * H0, count) + row, f32),
            pltpu.VMEM((ny + 2 * H0 - 2, count) + row, f32),
            pltpu.VMEM((ny + 4, count) + row, f32),
            pltpu.VMEM((ny + 2, count) + row, f32),
            pltpu.VMEM((ny + 2 * H0,) + row, f32),
            pltpu.VMEM((ny + 2 * H0 - 2,) + row, f32),
            pltpu.VMEM((ny + 2 * H0 - 2,) + row, f32),
            pltpu.VMEM((ny + 2 * H0 - 1,) + row, f32),
            pltpu.VMEM((ny,) + row, f32),
            pltpu.VMEM((ny,) + row, f32),
            pltpu.VMEM((nparam, ny // own) + row, f32),
            pltpu.VMEM((nparam, ny // own) + row, f32),
            pltpu.VMEM((ny + 2 * H0 - 2,) + row, f32),
            pltpu.VMEM((ny + 2,) + row, f32),
            dma((3,)),
            dma((2,)), dma((2,)),
            dma((2, H0)), dma((2, H0)),
            dma((2, 2)), dma((2, 2)),
        ] + sums,
        compiler_params=pltpu.CompilerParams(
            collective_id=0, has_side_effects=True, vmem_limit_bytes=60 << 20),
        cost_estimate=pl.CostEstimate(flops=12_000_000, bytes_accessed=1_200_000, transcendentals=0),
    )(
        grain_param.reshape(cx * ny, nz),
        perturbation.reshape(count * cx * ny, nz),
        mobility.reshape(cx * ny, nz),
    )
    return out.reshape(perturbation.shape)


def solution(mesh):
    nspace, nparam = mesh.shape["space"], mesh.shape["param"]
    in_specs = (
        P("space", None, None, None),
        P("param", "space", None, None, None),
        P("space", None, None, None),
    )
    out_specs = P("param", "space", None, None, None)
    return jax.shard_map(
        functools.partial(local, nspace, nparam), mesh=mesh, in_specs=in_specs, out_specs=out_specs, check_vma=False)
```

```python
import functools
import jax
import jax.numpy as jnp
from jax import lax
from jax.experimental import pallas as pl
from jax.experimental.pallas import tpu as pltpu
from jax.sharding import PartitionSpec as P

MESH = pl.DeviceIdType.MESH
DT = 0.05
H0 = 2
OWNERS = (2, 3, 4, 5)
OUT_PARTS = 4


def kernel(nspace, nparam, g_hbm, u_hbm, m_hbm, out_hbm, *scratch):
    (out, out_sem, G, U, MI, F0, F1, F2, F3, M, HX, HZ, HY, S0, S1, RS0, RS1, T0, T1,
     in_sem, m_s, m_r, h0_s, h0_r, h2_s, h2_r,
     rs0_s, rs0_r, rs1_s, rs1_r, ag0_s, ag0_r, ag1_s, ag1_r, ex0_s, ex0_r, ex1_s, ex1_r) = scratch
    cx, ny, nz = 8, 8, 128
    count = F0.shape[1]
    own = len(OWNERS)
    span = ny // own
    s = lax.axis_index("space")
    p = lax.axis_index("param")
    up = lax.rem(s + 1, nspace)
    down = lax.rem(s + nspace - 1, nspace)
    sides = (s < nspace - 1, s > 0)
    up_count = jnp.where(sides[0], 1, 0)
    down_count = jnp.where(sides[1], 1, 0)

    loads = [
        pltpu.make_async_copy(g_hbm, G, in_sem.at[0]),
        pltpu.make_async_copy(m_hbm, MI, in_sem.at[1]),
        pltpu.make_async_copy(u_hbm, U, in_sem.at[2]),
    ]
    for load in loads:
        load.start()

    barrier = pltpu.get_barrier_semaphore()

    def greet(device):
        pl.semaphore_signal(barrier, inc=1, device_id=device, device_id_type=MESH)

    for k in range(1, nparam):
        greet((s, lax.rem(p + k, nparam)))

    @pl.when(sides[0])
    def _():
        greet((up, p))
        greet((up, OWNERS[0]))

    @pl.when(sides[1])
    def _():
        greet((down, p))
        greet((down, OWNERS[-1]))

    loads[0].wait()
    loads[1].wait()
    for j in range(ny):
        M[j + H0] = MI[pl.ds(j, cx, stride=ny), :]
    loads[2].wait()
    for j in range(ny):
        label = G[pl.ds(j, cx, stride=ny), :] - p * count
        total = None
        for q in range(count):
            value = U[pl.ds(q * cx * ny + j, cx, stride=ny), :]
            value = jnp.where(label == q, 1.0, 0.0) + value
            F0[j + H0, q] = value
            total = value * value if total is None else total + value * value
        S0[j] = total

    def blank(low, refs):
        for ref, halo in refs:
            for k in range(halo):
                row = ref.at[halo - 1 - k] if low else ref.at[halo + ny + k]
                row[...] = jnp.zeros_like(row)

    beyond = ((F0, H0), (F2, 2), (M, H0), (T0, H0 - 1), (T1, 1))

    @pl.when(jnp.logical_not(sides[1]))
    def _():
        blank(True, beyond)

    @pl.when(jnp.logical_not(sides[0]))
    def _():
        blank(False, beyond)

    heard = nparam - 1 + up_count + down_count
    heard = heard + jnp.where(p == OWNERS[0], nparam, 0) * down_count
    heard = heard + jnp.where(p == OWNERS[-1], nparam, 0) * up_count
    pl.semaphore_wait(barrier, heard)

    def remote(src, dst, send, recv, device):
        return pltpu.make_async_remote_copy(
            src_ref=src, dst_ref=dst, send_sem=send, recv_sem=recv,
            device_id=device, device_id_type=MESH)

    def start_sided(copies):
        for side in (0, 1):
            @pl.when(sides[side])
            def _():
                copies[side].start()

    def sent_sided(copies):
        for side in (0, 1):
            @pl.when(sides[side])
            def _():
                copies[side].wait_send()

    def arrived_sided(copies):
        for side in (0, 1):
            @pl.when(sides[1 - side])
            def _():
                copies[side].wait_recv()

    def reduce_copy(S, RS, ss, rr, i, slot):
        return remote(S.at[pl.ds(i * span, span)], RS.at[slot], ss.at[i], rr.at[slot], (s, OWNERS[i]))

    def reduce_start(S, RS, ss, rr, which=range(own)):
        for i in which:
            @pl.when(p != OWNERS[i])
            def _():
                reduce_copy(S, RS, ss, rr, i, p).start()

    def group_copy(T, edge, ss, rr, i, q):
        rows = T.at[pl.ds(edge + i * span, span)]
        return remote(rows, rows, ss.at[q], rr.at[i], (s, q))

    def edge_copy(T, edge, ss, rr, side, q):
        if side == 0:
            return remote(T.at[pl.ds(ny, edge)], T.at[pl.ds(0, edge)], ss.at[q], rr.at[0], (up, q))
        return remote(T.at[pl.ds(edge, edge)], T.at[pl.ds(edge + ny, edge)], ss.at[q], rr.at[1], (down, q))

    def finish_totals(S, RS, rs_s, rs_r, T, edge, ag_s, ag_r, ex_s, ex_r):
        for i in range(own):
            @pl.when(p == OWNERS[i])
            def _():
                total = S[pl.ds(i * span, span)]
                for q in range(nparam):
                    if q != OWNERS[i]:
                        reduce_copy(S, RS, rs_s, rs_r, i, q).wait_recv()
                        total = total + RS[q]
                T[pl.ds(edge + i * span, span)] = total
                if i == own - 1:
                    @pl.when(sides[0])
                    def _():
                        for q in range(nparam):
                            edge_copy(T, edge, ex_s, ex_r, 0, q).start()
                if i == 0:
                    @pl.when(sides[1])
                    def _():
                        for q in reversed(range(nparam)):
                            edge_copy(T, edge, ex_s, ex_r, 1, q).start()
                for d in reversed(range(1, nparam)):
                    for q in (OWNERS[i] - d, OWNERS[i] + d):
                        if 0 <= q < nparam:
                            group_copy(T, edge, ag_s, ag_r, i, q).start()

    def group_wait(T, edge, ag_s, ag_r):
        for i in range(own):
            @pl.when(p != OWNERS[i])
            def _():
                group_copy(T, edge, ag_s, ag_r, i, 0).wait_recv()

    def edge_wait(T, edge, ex_s, ex_r):
        arrived_sided([edge_copy(T, edge, ex_s, ex_r, side, 0) for side in (0, 1)])

    def settle(S, RS, rs_s, rs_r, T, edge, ag_s, ag_r, ex_s, ex_r):
        for i in range(own):
            @pl.when(p != OWNERS[i])
            def _():
                reduce_copy(S, RS, rs_s, rs_r, i, p).wait_send()

            @pl.when(p == OWNERS[i])
            def _():
                for q in range(nparam):
                    if q != OWNERS[i]:
                        group_copy(T, edge, ag_s, ag_r, i, q).wait_send()
                for side, j in ((0, own - 1), (1, 0)):
                    if i == j:
                        @pl.when(sides[side])
                        def _():
                            for q in range(nparam):
                                edge_copy(T, edge, ex_s, ex_r, side, q).wait_send()

    def halo_pair(F, halo, ss, rr, k):
        return (
            remote(F.at[halo + ny - 1 - k], F.at[halo - 1 - k], ss.at[0, k], rr.at[0, k], (up, p)),
            remote(F.at[halo + k], F.at[halo + ny + k], ss.at[1, k], rr.at[1, k], (down, p)),
        )

    mobility = (
        remote(M.at[pl.ds(ny, H0)], M.at[pl.ds(0, H0)], m_s.at[0], m_r.at[0], (up, p)),
        remote(M.at[pl.ds(H0, H0)], M.at[pl.ds(H0 + ny, H0)], m_s.at[1], m_r.at[1], (down, p)),
    )
    first = [halo_pair(F0, H0, h0_s, h0_r, k) for k in range(H0)]
    second = {k: halo_pair(F2, 2, h2_s, h2_r, k) for k in range(H0 - 2, 2)}

    sum0 = (S0, RS0, rs0_s, rs0_r, T0, H0 - 1, ag0_s, ag0_r, ex0_s, ex0_r)
    sum1 = (S1, RS1, rs1_s, rs1_r, T1, 1, ag1_s, ag1_r, ex1_s, ex1_r)

    reduce_start(S0, RS0, rs0_s, rs0_r)
    start_sided(mobility)
    start_sided(first[0])

    start_sided(first[1])

    below = jnp.where(s > 0, 0.5 * DT, 0.0)
    above = jnp.where(s < nspace - 1, 0.5 * DT, 0.0)
    inner_x = jnp.where(lax.broadcasted_iota(jnp.int32, (cx, nz), 0) < cx - 1, 0.5 * DT, 0.0)
    inner_z = jnp.where(lax.broadcasted_iota(jnp.int32, (cx, nz), 1) < nz - 1, 0.5 * DT, 0.0)

    def row_faces(y):
        m = M[y + H0]
        HX[y + H0 - 1] = inner_x * (m + pltpu.roll(m, cx - 1, 0))
        HZ[y + H0 - 1] = inner_z * (m + pltpu.roll(m, nz - 1, 1))

    def column_face(y):
        scale = below if y == -1 else above if y == ny - 1 else 0.5 * DT
        HY[y + H0] = scale * (M[y + H0] + M[y + H0 + 1])

    for y in range(ny):
        row_faces(y)
    for y in range(ny - 1):
        column_face(y)

    def advance(src, so, store, T, edge, lo, hi, S=None, fields=None):
        def row(y, carry):
            m = M[y + H0]
            linear = 1.0 - (DT * m) * (3.0 * T[y + edge] - 1.0)
            square = (2.0 * DT) * m
            hx = HX[y + H0 - 1]
            hz = HZ[y + H0 - 1]
            hu = HY[y + H0]
            hl = HY[y + H0 - 1]
            total = None
            for q in fields or range(count):
                f = src[y + so, q]
                gx = hx * (pltpu.roll(f, cx - 1, 0) - f)
                gz = hz * (pltpu.roll(f, nz - 1, 1) - f)
                flow = hu * (src[y + so + 1, q] - f) - hl * (f - src[y + so - 1, q])
                flow = flow + ((gx - pltpu.roll(gx, 1, 0)) + (gz - pltpu.roll(gz, 1, 1)))
                value = f * (linear + square * (f * f)) + flow
                store(y, q, value)
                if S is not None:
                    total = value * value if total is None else total + value * value
            if S is not None:
                S[y] = total
            return carry

        if hi - lo == 1:
            row(lo, 0)
        else:
            lax.fori_loop(lo, hi, row, 0)

    def into(F, halo):
        def store(y, q, value):
            F[y + halo, q] = value
        return store

    def emit(y, q, value):
        out[pl.ds(q * cx * ny + y, cx, stride=ny), :] = 0.5 * value

    step1 = functools.partial(advance, F0, H0, into(F1, H0 - 1), T0, H0 - 1)
    step2 = functools.partial(advance, F1, H0 - 1, into(F2, 2), T0, H0 - 1)
    step3 = functools.partial(advance, F2, 2, into(F3, 1), T1, 1)
    step4 = functools.partial(advance, F3, 1, emit, T1, 1)

    finish_totals(*sum0)

    arrived_sided(mobility)
    for k in range(H0 - 1):
        row_faces(-1 - k)
        row_faces(ny + k)
    for k in range(H0):
        column_face(-1 - k)
        column_face(ny - 1 + k)

    group_wait(T0, H0 - 1, ag0_s, ag0_r)
    step1(1, ny - 1)
    step2(2, ny - 2, S1)
    reduce_start(S1, RS1, rs1_s, rs1_r, (1, 2))
    arrived_sided(first[0])
    step1(0, 1)
    step1(ny - 1, ny)
    step2(1, 2, S1)
    step2(ny - 2, ny - 1, S1)
    start_sided(second[1])
    edge_wait(T0, H0 - 1, ex0_s, ex0_r)
    arrived_sided(first[1])
    step1(-1, 0)
    step1(ny, ny + 1)
    step2(0, 1, S1)
    step2(ny - 1, ny, S1)

    reduce_start(S1, RS1, rs1_s, rs1_r, (0, 3))

    is_owner = functools.reduce(jnp.logical_or, [p == o for o in OWNERS])

    @pl.when(jnp.logical_not(is_owner))
    def _():
        start_sided(second[0])

    finish_totals(*sum1)

    @pl.when(is_owner)
    def _():
        start_sided(second[0])


    for k in range(2, H0):
        arrived_sided(first[k])
        step1(-k, 1 - k)
        step1(ny + k - 1, ny + k)
        step2(1 - k, 2 - k)
        step2(ny + k - 2, ny + k - 1)

    group_wait(T1, 1, ag1_s, ag1_r)
    step3(1, ny - 1)
    step4(2, ny - 2)
    if 0 in second:
        arrived_sided(second[0])
    step3(0, 1)
    step3(ny - 1, ny)
    step4(1, 2)
    step4(ny - 2, ny - 1)
    edge_wait(T1, 1, ex1_s, ex1_r)
    if 1 in second:
        arrived_sided(second[1])
    part = count // OUT_PARTS
    writes = []
    for c in range(OUT_PARTS):
        fields = range(c * part, (c + 1) * part)
        step3(-1, 0, fields=fields)
        step3(ny, ny + 1, fields=fields)
        step4(0, 1, fields=fields)
        step4(ny - 1, ny, fields=fields)
        run = pl.ds(c * part * cx * ny, part * cx * ny)
        write = pltpu.make_async_copy(out.at[run], out_hbm.at[run], out_sem.at[c])
        write.start()
        writes.append(write)

    for pair in [mobility] + first + list(second.values()):
        sent_sided(pair)
    settle(*sum0)
    settle(*sum1)
    for write in writes:
        write.wait()


def local(nspace, nparam, grain_param, perturbation, mobility):
    count, _, cx, ny, nz = perturbation.shape
    own = len(OWNERS)
    f32 = jnp.float32
    row = (cx, nz)
    hbm = pl.BlockSpec(memory_space=pltpu.HBM)
    dma = pltpu.SemaphoreType.DMA
    sums = [dma((own,)), dma((nparam,))] * 2 + [dma((nparam,)), dma((own,))] * 2 + [dma((nparam,)), dma((2,))] * 2
    out = pl.pallas_call(
        functools.partial(kernel, nspace, nparam),
        out_shape=jax.ShapeDtypeStruct((count * cx * ny, nz), f32),
        in_specs=[hbm] * 3,
        out_specs=hbm,
        scratch_shapes=[
            pltpu.VMEM((count * cx * ny, nz), f32),
            dma((OUT_PARTS,)),
            pltpu.VMEM((cx * ny, nz), jnp.int32),
            pltpu.VMEM((count * cx * ny, nz), f32),
            pltpu.VMEM((cx * ny, nz), f32),
            pltpu.VMEM((ny + 2 * H0, count) + row, f32),
            pltpu.VMEM((ny + 2 * H0 - 2, count) + row, f32),
            pltpu.VMEM((ny + 4, count) + row, f32),
            pltpu.VMEM((ny + 2, count) + row, f32),
            pltpu.VMEM((ny + 2 * H0,) + row, f32),
            pltpu.VMEM((ny + 2 * H0 - 2,) + row, f32),
            pltpu.VMEM((ny + 2 * H0 - 2,) + row, f32),
            pltpu.VMEM((ny + 2 * H0 - 1,) + row, f32),
            pltpu.VMEM((ny,) + row, f32),
            pltpu.VMEM((ny,) + row, f32),
            pltpu.VMEM((nparam, ny // own) + row, f32),
            pltpu.VMEM((nparam, ny // own) + row, f32),
            pltpu.VMEM((ny + 2 * H0 - 2,) + row, f32),
            pltpu.VMEM((ny + 2,) + row, f32),
            dma((3,)),
            dma((2,)), dma((2,)),
            dma((2, H0)), dma((2, H0)),
            dma((2, 2)), dma((2, 2)),
        ] + sums,
        compiler_params=pltpu.CompilerParams(
            collective_id=0, has_side_effects=True, vmem_limit_bytes=60 << 20),
        cost_estimate=pl.CostEstimate(flops=12_000_000, bytes_accessed=1_200_000, transcendentals=0),
    )(
        grain_param.reshape(cx * ny, nz),
        perturbation.reshape(count * cx * ny, nz),
        mobility.reshape(cx * ny, nz),
    )
    return 2.0 * out.reshape(perturbation.shape)


def solution(mesh):
    nspace, nparam = mesh.shape["space"], mesh.shape["param"]
    in_specs = (
        P("space", None, None, None),
        P("param", "space", None, None, None),
        P("space", None, None, None),
    )
    out_specs = P("param", "space", None, None, None)
    return jax.shard_map(
        functools.partial(local, nspace, nparam), mesh=mesh, in_specs=in_specs, out_specs=out_specs, check_vma=False)
```

```python
import functools
import jax
import jax.numpy as jnp
from jax import lax
from jax.experimental import pallas as pl
from jax.experimental.pallas import tpu as pltpu
from jax.sharding import PartitionSpec as P

MESH = pl.DeviceIdType.MESH
DT = 0.05
H0 = 2
OWNERS = (2, 3, 4, 5)
OUT_PARTS = 4


def kernel(nspace, nparam, g_hbm, u_hbm, m_hbm, out_hbm, *scratch):
    (out, out_sem, G, U, MI, F0, F1, F2, F3, M, HX, HZ, HY, S0, S1, RS0, RS1, T0, T1,
     in_sem, m_s, m_r, h0_s, h0_r, h2_s, h2_r,
     rs0_s, rs0_r, rs1_s, rs1_r, ag0_s, ag0_r, ag1_s, ag1_r, ex0_s, ex0_r, ex1_s, ex1_r) = scratch
    cx, ny, nz = 8, 8, 128
    count = F0.shape[1]
    own = len(OWNERS)
    span = ny // own
    s = lax.axis_index("space")
    p = lax.axis_index("param")
    up = lax.rem(s + 1, nspace)
    down = lax.rem(s + nspace - 1, nspace)
    sides = (s < nspace - 1, s > 0)
    up_count = jnp.where(sides[0], 1, 0)
    down_count = jnp.where(sides[1], 1, 0)

    loads = [
        pltpu.make_async_copy(g_hbm, G, in_sem.at[0]),
        pltpu.make_async_copy(m_hbm, MI, in_sem.at[1]),
        pltpu.make_async_copy(u_hbm, U, in_sem.at[2]),
    ]
    for load in loads:
        load.start()

    barrier = pltpu.get_barrier_semaphore()

    def greet(device):
        pl.semaphore_signal(barrier, inc=1, device_id=device, device_id_type=MESH)

    for k in range(1, nparam):
        greet((s, lax.rem(p + k, nparam)))

    @pl.when(sides[0])
    def _():
        greet((up, p))
        greet((up, OWNERS[0]))

    @pl.when(sides[1])
    def _():
        greet((down, p))
        greet((down, OWNERS[-1]))

    loads[0].wait()
    loads[1].wait()
    for j in range(ny):
        M[j + H0] = MI[pl.ds(j, cx, stride=ny), :]
    loads[2].wait()
    for j in range(ny):
        label = G[pl.ds(j, cx, stride=ny), :] - p * count
        total = None
        for q in range(count):
            value = U[pl.ds(q * cx * ny + j, cx, stride=ny), :]
            value = jnp.where(label == q, 1.0, 0.0) + value
            F0[j + H0, q] = value
            total = value * value if total is None else total + value * value
        S0[j] = total

    def blank(low, refs):
        for ref, halo in refs:
            for k in range(halo):
                row = ref.at[halo - 1 - k] if low else ref.at[halo + ny + k]
                row[...] = jnp.zeros_like(row)

    beyond = ((F0, H0), (F2, 2), (M, H0), (T0, H0 - 1), (T1, 1))

    @pl.when(jnp.logical_not(sides[1]))
    def _():
        blank(True, beyond)

    @pl.when(jnp.logical_not(sides[0]))
    def _():
        blank(False, beyond)

    heard = nparam - 1 + up_count + down_count
    heard = heard + jnp.where(p == OWNERS[0], nparam, 0) * down_count
    heard = heard + jnp.where(p == OWNERS[-1], nparam, 0) * up_count
    pl.semaphore_wait(barrier, heard)

    def remote(src, dst, send, recv, device):
        return pltpu.make_async_remote_copy(
            src_ref=src, dst_ref=dst, send_sem=send, recv_sem=recv,
            device_id=device, device_id_type=MESH)

    def start_sided(copies):
        for side in (0, 1):
            @pl.when(sides[side])
            def _():
                copies[side].start()

    def sent_sided(copies):
        for side in (0, 1):
            @pl.when(sides[side])
            def _():
                copies[side].wait_send()

    def arrived_sided(copies):
        for side in (0, 1):
            @pl.when(sides[1 - side])
            def _():
                copies[side].wait_recv()

    def reduce_copy(S, RS, ss, rr, i, slot):
        return remote(S.at[pl.ds(i * span, span)], RS.at[slot], ss.at[i], rr.at[slot], (s, OWNERS[i]))

    def reduce_start(S, RS, ss, rr, which=range(own)):
        for i in which:
            @pl.when(p != OWNERS[i])
            def _():
                reduce_copy(S, RS, ss, rr, i, p).start()

    def group_copy(T, edge, ss, rr, i, q):
        rows = T.at[pl.ds(edge + i * span, span)]
        return remote(rows, rows, ss.at[q], rr.at[i], (s, q))

    def edge_copy(T, edge, ss, rr, side, q):
        if side == 0:
            return remote(T.at[pl.ds(ny, edge)], T.at[pl.ds(0, edge)], ss.at[q], rr.at[0], (up, q))
        return remote(T.at[pl.ds(edge, edge)], T.at[pl.ds(edge + ny, edge)], ss.at[q], rr.at[1], (down, q))

    def finish_totals(S, RS, rs_s, rs_r, T, edge, ag_s, ag_r, ex_s, ex_r):
        for i in range(own):
            @pl.when(p == OWNERS[i])
            def _():
                total = S[pl.ds(i * span, span)]
                for q in range(nparam):
                    if q != OWNERS[i]:
                        reduce_copy(S, RS, rs_s, rs_r, i, q).wait_recv()
                        total = total + RS[q]
                T[pl.ds(edge + i * span, span)] = total
                if i == own - 1:
                    @pl.when(sides[0])
                    def _():
                        for q in range(nparam):
                            edge_copy(T, edge, ex_s, ex_r, 0, q).start()
                if i == 0:
                    @pl.when(sides[1])
                    def _():
                        for q in reversed(range(nparam)):
                            edge_copy(T, edge, ex_s, ex_r, 1, q).start()
                for d in reversed(range(1, nparam)):
                    for q in (OWNERS[i] - d, OWNERS[i] + d):
                        if 0 <= q < nparam:
                            group_copy(T, edge, ag_s, ag_r, i, q).start()

    def group_wait(T, edge, ag_s, ag_r):
        for i in range(own):
            @pl.when(p != OWNERS[i])
            def _():
                group_copy(T, edge, ag_s, ag_r, i, 0).wait_recv()

    def edge_wait(T, edge, ex_s, ex_r):
        arrived_sided([edge_copy(T, edge, ex_s, ex_r, side, 0) for side in (0, 1)])

    def settle(S, RS, rs_s, rs_r, T, edge, ag_s, ag_r, ex_s, ex_r):
        for i in range(own):
            @pl.when(p != OWNERS[i])
            def _():
                reduce_copy(S, RS, rs_s, rs_r, i, p).wait_send()

            @pl.when(p == OWNERS[i])
            def _():
                for q in range(nparam):
                    if q != OWNERS[i]:
                        group_copy(T, edge, ag_s, ag_r, i, q).wait_send()
                for side, j in ((0, own - 1), (1, 0)):
                    if i == j:
                        @pl.when(sides[side])
                        def _():
                            for q in range(nparam):
                                edge_copy(T, edge, ex_s, ex_r, side, q).wait_send()

    def halo_pair(F, halo, ss, rr, k):
        return (
            remote(F.at[halo + ny - 1 - k], F.at[halo - 1 - k], ss.at[0, k], rr.at[0, k], (up, p)),
            remote(F.at[halo + k], F.at[halo + ny + k], ss.at[1, k], rr.at[1, k], (down, p)),
        )

    mobility = (
        remote(M.at[pl.ds(ny, H0)], M.at[pl.ds(0, H0)], m_s.at[0], m_r.at[0], (up, p)),
        remote(M.at[pl.ds(H0, H0)], M.at[pl.ds(H0 + ny, H0)], m_s.at[1], m_r.at[1], (down, p)),
    )
    first = [halo_pair(F0, H0, h0_s, h0_r, k) for k in range(H0)]
    second = {1: halo_pair(F2, 2, h2_s, h2_r, 1)}

    def near_half(c):
        half = count // 2
        part = F2.at[:, pl.ds(c * half, half)]
        slot = 2 * c
        return (
            remote(part.at[1 + ny], part.at[1], h2_s.at[0, slot], h2_r.at[0, slot], (up, p)),
            remote(part.at[2], part.at[2 + ny], h2_s.at[1, slot], h2_r.at[1, slot], (down, p)),
        )

    near = [near_half(c) for c in (0, 1)]

    sum0 = (S0, RS0, rs0_s, rs0_r, T0, H0 - 1, ag0_s, ag0_r, ex0_s, ex0_r)
    sum1 = (S1, RS1, rs1_s, rs1_r, T1, 1, ag1_s, ag1_r, ex1_s, ex1_r)

    reduce_start(S0, RS0, rs0_s, rs0_r)
    start_sided(mobility)
    start_sided(first[0])

    start_sided(first[1])

    below = jnp.where(s > 0, 0.5 * DT, 0.0)
    above = jnp.where(s < nspace - 1, 0.5 * DT, 0.0)
    inner_x = jnp.where(lax.broadcasted_iota(jnp.int32, (cx, nz), 0) < cx - 1, 0.5 * DT, 0.0)
    inner_z = jnp.where(lax.broadcasted_iota(jnp.int32, (cx, nz), 1) < nz - 1, 0.5 * DT, 0.0)

    def row_faces(y):
        m = M[y + H0]
        HX[y + H0 - 1] = inner_x * (m + pltpu.roll(m, cx - 1, 0))
        HZ[y + H0 - 1] = inner_z * (m + pltpu.roll(m, nz - 1, 1))

    def column_face(y):
        scale = below if y == -1 else above if y == ny - 1 else 0.5 * DT
        HY[y + H0] = scale * (M[y + H0] + M[y + H0 + 1])

    for y in range(ny):
        row_faces(y)
    for y in range(ny - 1):
        column_face(y)

    def advance(src, so, store, T, edge, lo, hi, S=None, fields=None):
        def row(y, carry):
            m = M[y + H0]
            linear = 1.0 - (DT * m) * (3.0 * T[y + edge] - 1.0)
            square = (2.0 * DT) * m
            hx = HX[y + H0 - 1]
            hz = HZ[y + H0 - 1]
            hu = HY[y + H0]
            hl = HY[y + H0 - 1]
            total = None
            for q in fields or range(count):
                f = src[y + so, q]
                gx = hx * (pltpu.roll(f, cx - 1, 0) - f)
                gz = hz * (pltpu.roll(f, nz - 1, 1) - f)
                flow = hu * (src[y + so + 1, q] - f) - hl * (f - src[y + so - 1, q])
                flow = flow + ((gx - pltpu.roll(gx, 1, 0)) + (gz - pltpu.roll(gz, 1, 1)))
                value = f * (linear + square * (f * f)) + flow
                store(y, q, value)
                if S is not None:
                    total = value * value if total is None else total + value * value
            if S is not None:
                S[y] = total
            return carry

        if hi - lo == 1:
            row(lo, 0)
        else:
            lax.fori_loop(lo, hi, row, 0)

    def into(F, halo):
        def store(y, q, value):
            F[y + halo, q] = value
        return store

    def emit(y, q, value):
        out[pl.ds(q * cx * ny + y, cx, stride=ny), :] = value

    step1 = functools.partial(advance, F0, H0, into(F1, H0 - 1), T0, H0 - 1)
    step2 = functools.partial(advance, F1, H0 - 1, into(F2, 2), T0, H0 - 1)
    step3 = functools.partial(advance, F2, 2, into(F3, 1), T1, 1)
    step4 = functools.partial(advance, F3, 1, emit, T1, 1)

    finish_totals(*sum0)

    arrived_sided(mobility)
    for k in range(H0 - 1):
        row_faces(-1 - k)
        row_faces(ny + k)
    for k in range(H0):
        column_face(-1 - k)
        column_face(ny - 1 + k)

    group_wait(T0, H0 - 1, ag0_s, ag0_r)
    step1(1, ny - 1)
    step2(2, ny - 2, S1)
    reduce_start(S1, RS1, rs1_s, rs1_r, (1, 2))
    arrived_sided(first[0])
    step1(0, 1)
    step1(ny - 1, ny)
    step2(1, 2, S1)
    step2(ny - 2, ny - 1, S1)
    start_sided(second[1])
    edge_wait(T0, H0 - 1, ex0_s, ex0_r)
    arrived_sided(first[1])
    step1(-1, 0)
    step1(ny, ny + 1)
    step2(0, 1, S1)
    step2(ny - 1, ny, S1)

    reduce_start(S1, RS1, rs1_s, rs1_r, (0, 3))

    is_inner = functools.reduce(jnp.logical_or, [p == o for o in OWNERS[1:-1]])
    is_outer = jnp.logical_or(p == OWNERS[0], p == OWNERS[-1])
    is_owner = jnp.logical_or(is_inner, is_outer)

    @pl.when(jnp.logical_not(is_inner))
    def _():
        start_sided(near[0])

    @pl.when(jnp.logical_not(is_owner))
    def _():
        start_sided(near[1])

    finish_totals(*sum1)

    @pl.when(is_inner)
    def _():
        start_sided(near[0])

    @pl.when(is_owner)
    def _():
        start_sided(near[1])

    for k in range(2, H0):
        arrived_sided(first[k])
        step1(-k, 1 - k)
        step1(ny + k - 1, ny + k)
        step2(1 - k, 2 - k)
        step2(ny + k - 2, ny + k - 1)

    group_wait(T1, 1, ag1_s, ag1_r)
    step3(1, ny - 1)
    step4(2, ny - 2)
    for pair in near:
        arrived_sided(pair)
    step3(0, 1)
    step3(ny - 1, ny)
    step4(1, 2)
    step4(ny - 2, ny - 1)
    edge_wait(T1, 1, ex1_s, ex1_r)
    arrived_sided(second[1])
    part = count // OUT_PARTS
    writes = []
    for c in range(OUT_PARTS):
        fields = range(c * part, (c + 1) * part)
        step3(-1, 0, fields=fields)
        step3(ny, ny + 1, fields=fields)
        step4(0, 1, fields=fields)
        step4(ny - 1, ny, fields=fields)
        run = pl.ds(c * part * cx * ny, part * cx * ny)
        write = pltpu.make_async_copy(out.at[run], out_hbm.at[run], out_sem.at[c])
        write.start()
        writes.append(write)

    for pair in [mobility] + first + near + [second[1]]:
        sent_sided(pair)
    settle(*sum0)
    settle(*sum1)
    for write in writes:
        write.wait()


def local(nspace, nparam, grain_param, perturbation, mobility):
    count, _, cx, ny, nz = perturbation.shape
    own = len(OWNERS)
    f32 = jnp.float32
    row = (cx, nz)
    hbm = pl.BlockSpec(memory_space=pltpu.HBM)
    dma = pltpu.SemaphoreType.DMA
    sums = [dma((own,)), dma((nparam,))] * 2 + [dma((nparam,)), dma((own,))] * 2 + [dma((nparam,)), dma((2,))] * 2
    out = pl.pallas_call(
        functools.partial(kernel, nspace, nparam),
        out_shape=jax.ShapeDtypeStruct((count * cx * ny, nz), f32),
        in_specs=[hbm] * 3,
        out_specs=hbm,
        scratch_shapes=[
            pltpu.VMEM((count * cx * ny, nz), f32),
            dma((OUT_PARTS,)),
            pltpu.VMEM((cx * ny, nz), jnp.int32),
            pltpu.VMEM((count * cx * ny, nz), f32),
            pltpu.VMEM((cx * ny, nz), f32),
            pltpu.VMEM((ny + 2 * H0, count) + row, f32),
            pltpu.VMEM((ny + 2 * H0 - 2, count) + row, f32),
            pltpu.VMEM((ny + 4, count) + row, f32),
            pltpu.VMEM((ny + 2, count) + row, f32),
            pltpu.VMEM((ny + 2 * H0,) + row, f32),
            pltpu.VMEM((ny + 2 * H0 - 2,) + row, f32),
            pltpu.VMEM((ny + 2 * H0 - 2,) + row, f32),
            pltpu.VMEM((ny + 2 * H0 - 1,) + row, f32),
            pltpu.VMEM((ny,) + row, f32),
            pltpu.VMEM((ny,) + row, f32),
            pltpu.VMEM((nparam, ny // own) + row, f32),
            pltpu.VMEM((nparam, ny // own) + row, f32),
            pltpu.VMEM((ny + 2 * H0 - 2,) + row, f32),
            pltpu.VMEM((ny + 2,) + row, f32),
            dma((3,)),
            dma((2,)), dma((2,)),
            dma((2, H0)), dma((2, H0)),
            dma((2, 3)), dma((2, 3)),
        ] + sums,
        compiler_params=pltpu.CompilerParams(
            collective_id=0, has_side_effects=True, vmem_limit_bytes=60 << 20),
        cost_estimate=pl.CostEstimate(flops=12_000_000, bytes_accessed=1_200_000, transcendentals=0),
    )(
        grain_param.reshape(cx * ny, nz),
        perturbation.reshape(count * cx * ny, nz),
        mobility.reshape(cx * ny, nz),
    )
    return out.reshape(perturbation.shape)


def solution(mesh):
    nspace, nparam = mesh.shape["space"], mesh.shape["param"]
    in_specs = (
        P("space", None, None, None),
        P("param", "space", None, None, None),
        P("space", None, None, None),
    )
    out_specs = P("param", "space", None, None, None)
    return jax.shard_map(
        functools.partial(local, nspace, nparam), mesh=mesh, in_specs=in_specs, out_specs=out_specs, check_vma=False)
```
